256 devices in a mesh: depth: 16 (over x, z_lo), gx: 16 (over z_hi, y, core).
Axes of the slice: x: 4, y: 4, z: 8 (z_hi: 2, z_lo: 4; z = z_hi * 4 + z_lo), core: 2. Of those that a mesh axis runs over, the one named last changes fastest.
Arguments:
- volume: bfloat16 [64, 384, 2, 2048], P(None, 'depth', None, 'gx'), may hold values from -6 to 6
- conv_first: bfloat16 [3, 3, 3, 64, 64], replicated, may hold values from -0.15625 to 0.15625
- conv_second: bfloat16 [3, 3, 3, 64, 64], replicated, may hold values from -0.15625 to 0.15625
- mode_weights: bfloat16 [64, 64, 64], P('depth'), may hold values from -0.75 to 0.75
Outputs:
- next_volume: bfloat16 [64, 384, 2, 2048], P(None, 'depth', None, 'gx')
The draws below stay inside these ranges and needn't reach their ends.
All inputs are finite; a program needn't handle non-finite values.
Results may differ from the reference program's by a relative error of at most 0.01.
Values may be sent and summed in bfloat16 or wider, within the bound.
A program may use at most 64 MiB of HBM per device.

```python
import math
import jax
import jax.numpy as jnp
from jax import lax

C = 64
MODES = 32
CD = 24
NY = 2
NZ = 384
NX = 2048
N_DEPTH = 16


def levels(key, dims, split, low, high):
    def one(position, parts):
        steps = jax.random.uniform(jax.random.fold_in(jax.random.fold_in(key, 6), position), (parts,), jnp.float32, low / len(split), high / len(split))
        return jnp.repeat(jnp.exp(steps), dims[position] // parts).reshape((-1,) + (1,) * (len(dims) - position - 1))

    factor_of = one(*split[0])
    for cut in split[1:]:
        factor_of = factor_of * one(*cut)
    return factor_of


def scatter_about(own_key, extent, scale, limit, pieces=(), kind=jnp.bfloat16):
    gain = levels(own_key, extent, pieces, -0.22, 0.18) if pieces else 1.0
    array = jax.random.normal(own_key, extent, jnp.float32) * scale * gain
    return jnp.minimum(jnp.maximum(array, -limit), limit).astype(kind)


def setup_inputs(seed: int = 0) -> dict:
    seeds = jax.random.split(jax.random.key(seed), 5)
    return {
        "volume": scatter_about(seeds[0], (C, NZ, NY, NX), 1.0, 6.0, ((1, 16), (3, 16))),
        "conv_first": scatter_about(seeds[1], (3, 3, 3, C, C), (27 * C) ** -0.5, 0.15625),
        "conv_second": scatter_about(seeds[2], (3, 3, 3, C, C), (27 * C) ** -0.5, 0.15625),
        "mode_weights": scatter_about(seeds[3], (2 * MODES, C, C), C ** -0.5, 0.75, ((0, 16),)),
    }


def mode_basis(mode_index, depth_pos, total_z):
    frequency = jnp.where(mode_index < MODES, mode_index, mode_index - MODES + 1).astype(jnp.float32)
    odd_steps = (2 * depth_pos + 1).astype(jnp.float32)
    angles = frequency[:, None] * odd_steps[None, :] * (math.pi / (2.0 * total_z))
    values = jnp.where((mode_index < MODES)[:, None], jnp.cos(angles), jnp.sin(angles))
    return (values * math.sqrt(2.0 / total_z)).astype(jnp.bfloat16)

def convolve(source, weights):
    kernel = jnp.transpose(weights.astype(jnp.float32), (3, 4, 0, 1, 2))
    result = lax.conv_general_dilated(source[None].astype(jnp.float32), kernel, (1, 1, 1), 'SAME', dimension_numbers=('NCDHW', 'OIDHW', 'NCDHW'), precision=lax.Precision.HIGHEST)
    return result[0]

def reference(volume, conv_first, conv_second, mode_weights):
    hidden = jax.nn.gelu(convolve(volume, conv_first)).astype(jnp.bfloat16)
    local_part = convolve(hidden, conv_second)
    mode_index = jnp.arange(2 * MODES, dtype=jnp.int32)

    def shard_term(running, shard_index):
        depth_pos = shard_index * CD + jnp.arange(CD, dtype=jnp.int32)
        slab = lax.dynamic_slice_in_dim(volume, (shard_index * CD).astype(jnp.int32), CD, 1)
        partial_term = jnp.einsum('mz,czyx->mcyx', mode_basis(mode_index, depth_pos, NZ).astype(jnp.float32), slab.astype(jnp.float32), precision=lax.Precision.HIGHEST)
        rounded = lax.optimization_barrier(partial_term.astype(jnp.bfloat16))
        return (running + rounded.astype(jnp.float32), None)
    start_sum = jnp.zeros((2 * MODES, C, NY, volume.shape[3]), jnp.float32)
    summed, _ = lax.scan(shard_term, start_sum, jnp.arange(N_DEPTH, dtype=jnp.int32))
    coefficients = summed.astype(jnp.bfloat16)
    mixed = jnp.einsum('moc,mcyx->moyx', mode_weights.astype(jnp.float32), coefficients.astype(jnp.float32), precision=lax.Precision.HIGHEST).astype(jnp.bfloat16)
    full_basis = mode_basis(mode_index, jnp.arange(NZ, dtype=jnp.int32), NZ).astype(jnp.float32)
    spectral = jnp.einsum('mz,mcyx->czyx', full_basis, mixed.astype(jnp.float32), precision=lax.Precision.HIGHEST)
    return (volume.astype(jnp.float32) + local_part + spectral).astype(jnp.bfloat16)
```

```python
import math

import jax
import jax.numpy as jnp
import ml_dtypes
import numpy as np
from jax import lax
from jax.experimental import pallas as pl
from jax.experimental.pallas import tpu as pltpu
from jax.sharding import PartitionSpec as P

MODES = 32
M = 2 * MODES
C = 64
ROWS = 128
LANES = 128
CD = 24
NZ = 384
ND = 16
NG = 16
R = 10
XO = LANES // ND
GROUP = 8
MESH = pl.DeviceIdType.MESH
F32 = jnp.float32
BF16 = jnp.bfloat16


def slab_factors():
    mode = np.arange(M)
    k = np.where(mode < MODES, mode, mode - MODES + 1)
    t = k[:, None] * (2 * np.arange(NZ)[None, :] + 1) * (math.pi / (2 * NZ))
    basis = math.sqrt(2.0 / NZ) * np.where((mode < MODES)[:, None], np.cos(t), np.sin(t))
    z = np.arange(CD) - (CD - 1) / 2
    a = np.arange(MODES + 1)[:, None] * z[None, :] * (math.pi / NZ)
    h = np.linalg.svd(np.concatenate([np.cos(a), np.sin(a)]))[2][:R]
    g = np.einsum("msz,rz->msr", basis.reshape(M, ND, CD), h)
    return g.reshape(M, ND * R), h


def constants():
    g, h = slab_factors()
    hk = np.kron(h, np.eye(16)).astype(ml_dtypes.bfloat16)
    gk = np.kron(g, np.eye(XO)).astype(ml_dtypes.bfloat16)
    return hk, np.ascontiguousarray(hk.T), gk, np.ascontiguousarray(gk.T)


def dot(a, b, ca=1, cb=0):
    return lax.dot_general(a, b, (((ca,), (cb,)), ((), ())), preferred_element_type=F32)


def iota(shape, dim):
    return lax.broadcasted_iota(jnp.int32, shape, dim)


def one_hot(mask):
    return jnp.where(mask, 1.0, 0.0).astype(BF16)


def gelu(x):
    inner = math.sqrt(2.0 / math.pi) * (x + 0.044715 * (x * x * x))
    return 0.5 * x * (1.0 + jnp.tanh(inner))


def kernel(
    vol_h, w1_h, w2_h, mw_h, hk_h, hkt_h, gk_h, gkt_h, out,
    vol, wc1, wc2, mw, hk, hkt, gk, gkt,
    vs, hs, wa, wb, acc, eb, rx,
    gb, fs, fr, bs, br, coef, mixed,
    pw, wp, wall, bd,
    load_sem, vol_sem, fss, frs, bss, brs, pss, prs, qss, qrs, hss, hrs,
):
    d = lax.axis_index("depth")
    g = lax.axis_index("gx")
    q = lax.rem(g, GROUP)
    gbase = g - q

    def depth_peer(k):
        return lax.rem(d + k, ND)

    def group_peer(k):
        return gbase + lax.rem(q + k, GROUP)

    loads = [
        pltpu.make_async_copy(s, t, load_sem.at[i])
        for i, (s, t) in enumerate(
            [(mw_h, mw), (hk_h, hk), (w1_h, wc1), (gk_h, gk), (w2_h, wc2), (gkt_h, gkt), (hkt_h, hkt)]
        )
    ]

    def vol_load(z):
        return pltpu.make_async_copy(vol_h.at[:, z], vol.at[z], vol_sem.at[z])

    loads[0].start()
    loads[1].start()

    def start_vol(z, _):
        vol_load(z).start()
        return 0

    lax.fori_loop(0, CD, start_vol, 0)
    for c in loads[2:]:
        c.start()

    barrier = pltpu.get_barrier_semaphore()

    def greet(dd, gg):
        pl.semaphore_signal(barrier, 1, device_id=(dd, gg), device_id_type=MESH)

    def greet_depth(k, _):
        greet(depth_peer(k), g)
        return 0

    lax.fori_loop(1, ND, greet_depth, 0)

    def greet_group(k, _):
        greet(d, group_peer(k))
        return 0

    lax.fori_loop(1, GROUP, greet_group, 0)
    up, down = lax.rem(d + 1, ND), lax.rem(d + ND - 1, ND)
    right, left = lax.rem(g + 1, NG), lax.rem(g + NG - 1, NG)
    greet(d, right)
    greet(d, left)
    for dd in (up, down):
        for gg in (right, left):
            greet(dd, gg)

    row = iota((ROWS, LANES), 0)
    lane = iota((ROWS, LANES), 1)
    eye = one_hot(row == lane)
    perm = one_hot(lane == (row & 1) * C + (row >> 1))
    permt = one_hot(row == (lane & 1) * C + (lane >> 1))

    loads[0].wait()
    eye64 = eye[:C, :C]
    for p in range(2):
        two = mw[2 * p : 2 * p + 2].reshape(2 * C, C)
        pw[C * p : C * (p + 1), :] = dot(eye64, two, 1, 1).astype(BF16)
    piece = pl.ds(pl.multiple_of(q * 16, 16), 16)
    wp[d] = pw[piece, :]

    loads[1].wait()

    def wait_vol(z, _):
        vol_load(z).wait()
        return 0

    lax.fori_loop(0, CD, wait_vol, 0)
    flat = vol.reshape(CD, ROWS, LANES)

    def compress(i, _):
        r0 = pl.multiple_of(i * 32, 32)
        both = [flat[:, pl.ds(r0 + 16 * j, 16), :].reshape(CD * 16, LANES) for j in range(2)]
        res = dot(hk[...], jnp.concatenate(both, axis=1)).astype(BF16)
        for j in range(2):
            gb[:, pl.ds(r0 + 16 * j, 16), :] = res[:, LANES * j : LANES * (j + 1)].reshape(R, 16, LANES)
        return 0

    lax.fori_loop(0, ROWS // 32, compress, 0)

    for p in range(R // 2):
        pair = [dot(gb[2 * p + j], perm, 0, 0).reshape(ND, XO, LANES) for j in range(2)]
        fs[:, 16 * p : 16 * p + 16, :] = jnp.concatenate(pair, axis=1).astype(BF16)
    fr[d] = fs[d]
    vs[1, ROWS : 2 * ROWS, :] = flat[0]
    vs[CD, ROWS : 2 * ROWS, :] = flat[CD - 1]

    pl.semaphore_wait(barrier, ND - 1 + GROUP - 1 + 2 + 4)

    def piece_copy(k):
        t = depth_peer(k)
        return pltpu.make_async_remote_copy(
            pw.at[piece, :], wp.at[d], pss.at[k], prs.at[k], device_id=(t, g), device_id_type=MESH
        )

    def forward_copy(k):
        t = depth_peer(k)
        return pltpu.make_async_remote_copy(
            fs.at[t], fr.at[d], fss.at[k], frs.at[k], device_id=(t, g), device_id_type=MESH
        )

    def back_copy(k):
        t = depth_peer(k)
        return pltpu.make_async_remote_copy(
            bs.at[t], br.at[d], bss.at[k], brs.at[k], device_id=(t, g), device_id_type=MESH
        )

    def gather_copy(k):
        return pltpu.make_async_remote_copy(
            wp, wall.at[q], qss.at[k], qrs.at[k], device_id=(d, group_peer(k)), device_id_type=MESH
        )

    def slab_copies(n, ts):
        mid = pl.ds(ROWS, ROWS)
        for i, (src, dst, dd) in enumerate([(1, CD + 1, down), (CD, 0, up)]):
            yield pltpu.make_async_remote_copy(
                ts.at[src, mid, :], ts.at[dst, mid, :], hss.at[n, i], hrs.at[n, i], device_id=(dd, g), device_id_type=MESH
            )

    def edge_copies(n):
        i = 2
        for side, gg in ((0, left), (1, right)):
            base = 64 * (1 - side)
            for src, rows, dst, dd in ((0, 32, 0, d), (16, 16, 32, up), (0, 16, 48, down)):
                yield pltpu.make_async_remote_copy(
                    eb.at[n, pl.ds(32 * side + src, rows), :],
                    rx.at[n, pl.ds(base + dst, rows), :],
                    hss.at[n, i],
                    hrs.at[n, i],
                    device_id=(dd, gg),
                    device_id_type=MESH,
                )
                i += 1

    def run(lo, hi, make, what):
        def step(k, _):
            getattr(make(k), what)()
            return 0

        lax.fori_loop(lo, hi, step, 0)

    run(1, ND, piece_copy, "start")
    for c in slab_copies(0, vs):
        c.start()
    run(1, ND, forward_copy, "start")

    erow = iota((64, LANES), 0)
    elane = iota((64, LANES), 1)

    def edges_of(z, slab):
        pick = ((erow == z) & (elane == 0)) | ((erow == z + 32) & (elane == LANES - 1))
        return dot(one_hot(pick), slab, 1, 1)

    def spread(ts, zi, slab):
        ts[zi, 0:ROWS, :] = pltpu.roll(slab, 1, 1)
        ts[zi, ROWS : 2 * ROWS, :] = slab
        ts[zi, 2 * ROWS : 3 * ROWS, :] = pltpu.roll(slab, LANES - 1, 1)

    def fill(z, edge):
        slab = flat[z]
        spread(vs, z + 1, slab)
        acc[z] = slab.astype(F32)
        return edge + edges_of(z, slab)

    for z in (0, CD - 1):
        slab = flat[z]
        vs[z + 1, 0:ROWS, :] = pltpu.roll(slab, 1, 1)
        vs[z + 1, 2 * ROWS : 3 * ROWS, :] = pltpu.roll(slab, LANES - 1, 1)
        acc[z] = slab.astype(F32)
    edge = edges_of(0, flat[0]) + edges_of(CD - 1, flat[CD - 1])
    eb[0] = lax.fori_loop(1, CD - 1, fill, edge).astype(BF16)
    for c in edge_copies(0):
        c.start()

    loads[2].wait()
    loads[4].wait()

    def taps(t, _):
        a, e = t // 3, lax.rem(t, 3)

        def halves(w):
            w0, w1, w2 = w[a, 0, e], w[a, 1, e], w[a, 2, e]
            return jnp.concatenate([w1, w0], axis=0), jnp.concatenate([w2, w1], axis=0)

        lo, hi = halves(wc1)
        wa[t] = (dot(lo, permt[:C]) + dot(hi, permt[C:])).astype(BF16)
        lo, hi = halves(wc2)
        both = (dot(lo, eye[:C]) + dot(hi, eye[C:])).astype(BF16)
        wb[t] = dot(perm, both).astype(BF16)
        return 0

    lax.fori_loop(0, 9, taps, 0)

    run(1, ND, piece_copy, "wait")
    wall[q] = wp[...]
    run(1, GROUP, gather_copy, "start")

    def complete(n, ts):
        for c in slab_copies(n, ts):
            c.wait()
        for c in edge_copies(n):
            c.wait()
        for zi, there in ((0, d > 0), (CD + 1, d < ND - 1)):
            slab = ts[zi, ROWS : 2 * ROWS, :].astype(F32) * jnp.where(there, 1.0, 0.0)
            spread(ts, zi, slab.astype(BF16))
        sub = row & 63
        inside = jnp.where(row < 64, g, NG - 1 - g)
        slabs = jnp.where(sub < 32, 1, jnp.where(sub < 48, d, ND - 1 - d))
        keep = jnp.minimum(inside, slabs) > 0
        cells = jnp.where(keep, rx[n].astype(F32), 0.0).astype(BF16)
        columns = dot(eye, cells, 1, 1).astype(BF16)
        wrow = iota((ROWS, 2 * LANES), 0)
        wlane = iota((ROWS, 2 * LANES), 1)

        def patch(zi, _):
            rho = jnp.where(zi == 0, 39, jnp.where(zi == CD + 1, 48, zi - 1))
            put = ((wrow == rho) & (wlane == 0)) | ((wrow == rho + 64) & (wlane == 2 * LANES - 1))
            ins = dot(columns, one_hot(put)).astype(BF16)
            ts[zi, 0:ROWS, :] = jnp.where(lane == 0, ins[:, :LANES], ts[zi, 0:ROWS, :])
            ts[zi, 2 * ROWS : 3 * ROWS, :] = jnp.where(
                lane == LANES - 1, ins[:, LANES:], ts[zi, 2 * ROWS : 3 * ROWS, :]
            )
            return 0

        lax.fori_loop(0, CD + 2, patch, 0)

    def conv_pair(w, ts, z):
        lhs = jnp.concatenate([w[t] for t in range(9)], axis=1)
        rhs = [ts[pl.ds(z + j, 3)].reshape(9 * ROWS, LANES) for j in range(2)]
        return dot(lhs, jnp.concatenate(rhs, axis=1))

    complete(0, vs)

    def first(i, edge):
        z = 2 * i
        hidden = gelu(conv_pair(wa, vs, z)).astype(BF16)
        for j in range(2):
            slab = hidden[:, LANES * j : LANES * (j + 1)]
            spread(hs, z + j + 1, slab)
            edge = edge + edges_of(z + j, slab)
        return edge

    eb[1] = lax.fori_loop(0, CD // 2, first, jnp.zeros((64, LANES), F32)).astype(BF16)
    for c in slab_copies(1, hs):
        c.start()
    for c in edge_copies(1):
        c.start()

    run(1, GROUP, gather_copy, "wait")
    half = iota((C, LANES), 1) < C

    def diagonal(i, _):
        owner, p = i // 2, lax.rem(i, 2)
        w = wall[pl.ds(4 * p, 4), owner].reshape(C, LANES).astype(F32)
        turned = pltpu.roll(w, C, 1)
        top = [jnp.where(half, w, 0.0), jnp.where(half, turned, 0.0)]
        bottom = [jnp.where(half, 0.0, turned), jnp.where(half, 0.0, w)]
        bd[i, 0:C, :] = jnp.concatenate(top, axis=1).astype(BF16)
        bd[i, C : 2 * C, :] = jnp.concatenate(bottom, axis=1).astype(BF16)
        return 0

    lax.fori_loop(0, M // 2, diagonal, 0)

    loads[3].wait()
    loads[5].wait()
    run(1, ND, forward_copy, "wait")
    coef[...] = dot(gk[...], fr[...].reshape(ND * R * XO, LANES)).astype(BF16)

    def mix(i, _):
        rows = pl.ds(pl.multiple_of(16 * i, 16), 16)
        res = dot(coef[rows, :], bd[i])
        mixed[rows, :] = jnp.concatenate([res[:8, :LANES], res[8:, LANES:]], axis=0).astype(BF16)
        return 0

    lax.fori_loop(0, M // 2, mix, 0, unroll=4)
    bs[...] = dot(gkt[...], mixed[...]).astype(BF16).reshape(ND, R * XO, LANES)
    br[d] = bs[d]
    run(1, ND, back_copy, "start")

    complete(1, hs)

    def second(i, _):
        z = 2 * i
        res = conv_pair(wb, hs, z)
        for j in range(2):
            acc[z + j] += res[:, LANES * j : LANES * (j + 1)]
        return 0

    lax.fori_loop(0, CD // 2, second, 0)

    loads[6].wait()
    run(1, ND, back_copy, "wait")
    for p in range(R // 2):
        pair = br[:, 16 * p : 16 * p + 16, :].astype(F32)
        for j in range(2):
            cols = pair[:, XO * j : XO * (j + 1)].reshape(LANES, ROWS).astype(BF16)
            gb[2 * p + j] = dot(perm, cols, 1, 1).astype(BF16)

    def expand(i, _):
        r0 = pl.multiple_of(i * 32, 32)
        both = [gb[:, pl.ds(r0 + 16 * j, 16), :].reshape(R * 16, LANES) for j in range(2)]
        res = dot(hkt[...], jnp.concatenate(both, axis=1))
        for j in range(2):
            rows = pl.ds(r0 + 16 * j, 16)
            total = acc[:, rows, :] + res[:, LANES * j : LANES * (j + 1)].reshape(CD, 16, LANES)
            out[:, rows, :] = total.astype(BF16)
        return 0

    lax.fori_loop(0, ROWS // 32, expand, 0)


def local(volume, conv_first, conv_second, mode_weights):
    vmem = pltpu.VMEM
    dma = pltpu.SemaphoreType.DMA
    hbm = pl.BlockSpec(memory_space=pl.ANY)
    res = pl.pallas_call(
        kernel,
        out_shape=jax.ShapeDtypeStruct((CD, ROWS, LANES), BF16),
        in_specs=[hbm] * 8,
        out_specs=pl.BlockSpec(memory_space=pltpu.VMEM),
        scratch_shapes=[
            vmem((CD, C, 2, LANES), BF16),
            vmem((3, 3, 3, C, C), BF16),
            vmem((3, 3, 3, C, C), BF16),
            vmem((4, C, C), BF16),
            vmem((R * 16, CD * 16), BF16),
            vmem((CD * 16, R * 16), BF16),
            vmem((M * XO, ND * R * XO), BF16),
            vmem((ND * R * XO, M * XO), BF16),
            vmem((CD + 2, 3 * ROWS, LANES), BF16),
            vmem((CD + 2, 3 * ROWS, LANES), BF16),
            vmem((9, ROWS, LANES), BF16),
            vmem((9, ROWS, LANES), BF16),
            vmem((CD, ROWS, LANES), F32),
            vmem((2, 64, LANES), BF16),
            vmem((2, ROWS, LANES), BF16),
            vmem((R, ROWS, LANES), BF16),
            vmem((ND, R * XO, LANES), BF16),
            vmem((ND, R * XO, LANES), BF16),
            vmem((ND, R * XO, LANES), BF16),
            vmem((ND, R * XO, LANES), BF16),
            vmem((M * XO, LANES), BF16),
            vmem((M * XO, LANES), BF16),
            vmem((2 * C, LANES), BF16),
            vmem((ND, 16, LANES), BF16),
            vmem((GROUP, ND, 16, LANES), BF16),
            vmem((M // 2, ROWS, 2 * LANES), BF16),
            dma((7,)),
            dma((CD,)),
            dma((ND,)),
            dma((ND,)),
            dma((ND,)),
            dma((ND,)),
            dma((ND,)),
            dma((ND,)),
            dma((GROUP,)),
            dma((GROUP,)),
            dma((2, 8)),
            dma((2, 8)),
        ],
        compiler_params=pltpu.CompilerParams(
            collective_id=0, has_side_effects=True, vmem_limit_bytes=48 * 2**20
        ),
    )(volume, conv_first, conv_second, mode_weights, *constants())
    return res.reshape(CD, C, 2, LANES).transpose(1, 0, 2, 3)


def solution(mesh):
    placed = (P(None, "depth", None, "gx"), P(), P(), P("depth", None, None))
    return jax.shard_map(
        local, mesh=mesh, in_specs=placed, out_specs=P(None, "depth", None, "gx"), check_vma=False
    )
```

```python
import math

import jax
import jax.numpy as jnp
import ml_dtypes
import numpy as np
from jax import lax
from jax.experimental import pallas as pl
from jax.experimental.pallas import tpu as pltpu
from jax.sharding import PartitionSpec as P

MODES = 32
M = 2 * MODES
C = 64
ROWS = 128
LANES = 128
CD = 24
NZ = 384
ND = 16
NG = 16
R = 10
XO = LANES // ND
MESH = pl.DeviceIdType.MESH
F32 = jnp.float32
BF16 = jnp.bfloat16


def slab_factors():
    mode = np.arange(M)
    k = np.where(mode < MODES, mode, mode - MODES + 1)
    t = k[:, None] * (2 * np.arange(NZ)[None, :] + 1) * (math.pi / (2 * NZ))
    basis = math.sqrt(2.0 / NZ) * np.where((mode < MODES)[:, None], np.cos(t), np.sin(t))
    z = np.arange(CD) - (CD - 1) / 2
    a = np.arange(MODES + 1)[:, None] * z[None, :] * (math.pi / NZ)
    h = np.linalg.svd(np.concatenate([np.cos(a), np.sin(a)]))[2][:R]
    g = np.einsum("msz,rz->msr", basis.reshape(M, ND, CD), h)
    return g.reshape(M, ND * R), h


def constants():
    g, h = slab_factors()
    hk = np.kron(h, np.eye(16)).astype(ml_dtypes.bfloat16)
    gk = np.kron(g, np.eye(XO)).astype(ml_dtypes.bfloat16)
    return hk, np.ascontiguousarray(hk.T), gk, np.ascontiguousarray(gk.T)


def dot(a, b, ca=1, cb=0):
    return lax.dot_general(a, b, (((ca,), (cb,)), ((), ())), preferred_element_type=F32)


def iota(shape, dim):
    return lax.broadcasted_iota(jnp.int32, shape, dim)


def one_hot(mask):
    return jnp.where(mask, 1.0, 0.0).astype(BF16)


def gelu(x):
    inner = math.sqrt(2.0 / math.pi) * (x + 0.044715 * (x * x * x))
    return 0.5 * x * (1.0 + jnp.tanh(inner))


def kernel(
    vol_h, w1_h, w2_h, mw_h, hk_h, hkt_h, gk_h, gkt_h, out,
    vol, wc1, wc2, mw, hk, hkt, gk, gkt,
    vs, hs, wa, wb, acc, eb, rx,
    gb, fs, fr, bs, br, coef, mixed,
    wall, bd, res_out,
    load_sem, vol_sem, fss, frs, bss, brs, pss, prs, hss, hrs, out_sem,
):
    d = lax.axis_index("depth")
    g = lax.axis_index("gx")
    xd, zd = d // 4, lax.rem(d, 4)
    core = lax.rem(g, 2)
    half_z = zd // 2

    def depth_peer(k):
        return lax.rem(d + k, ND)

    def z_peer(k):
        return xd * 4 + lax.rem(zd + k, 4)

    def x_peer(k):
        return lax.rem(xd + k, 4) * 4 + zd

    def far_first(j):
        other = 1 - j // 8
        z = 2 * (half_z + other * (1 - 2 * half_z)) + lax.rem(zd + j + 1, 2)
        return lax.rem(xd + 1 + lax.rem(j, 8) // 2, 4) * 4 + z

    loads = [
        pltpu.make_async_copy(s, t, load_sem.at[i])
        for i, (s, t) in enumerate(
            [(mw_h, mw), (hk_h, hk), (w1_h, wc1), (gk_h, gk), (w2_h, wc2), (gkt_h, gkt), (hkt_h, hkt)]
        )
    ]

    def vol_load(z):
        return pltpu.make_async_copy(vol_h.at[:, z], vol.at[z], vol_sem.at[z])

    loads[0].start()
    loads[1].start()

    def start_vol(z, _):
        vol_load(z).start()
        return 0

    lax.fori_loop(0, CD, start_vol, 0)
    for c in loads[2:]:
        c.start()

    barrier = pltpu.get_barrier_semaphore()

    def greet(dd, gg):
        pl.semaphore_signal(barrier, 1, device_id=(dd, gg), device_id_type=MESH)

    def greet_depth(k, _):
        greet(depth_peer(k), g)
        return 0

    lax.fori_loop(1, ND, greet_depth, 0)

    twin = g + 1 - 2 * core
    greet(d, twin)
    up, down = lax.rem(d + 1, ND), lax.rem(d + ND - 1, ND)
    right, left = lax.rem(g + 1, NG), lax.rem(g + NG - 1, NG)
    greet(d, right)
    greet(d, left)
    for dd in (up, down):
        for gg in (right, left):
            greet(dd, gg)

    row = iota((ROWS, LANES), 0)
    lane = iota((ROWS, LANES), 1)
    eye = one_hot(row == lane)
    perm = one_hot(lane == (row & 1) * C + (row >> 1))
    permt = one_hot(row == (lane & 1) * C + (lane >> 1))

    loads[0].wait()
    two = mw[pl.ds(2 * core, 2)].reshape(2 * C, C)
    wall[core, xd, zd] = dot(eye[:C, :C], two, 1, 1).astype(BF16)

    def weights_copy(n, k):
        ref = [wall.at[core, xd, zd], wall.at[core, xd], wall.at[core]][n]
        to = [(z_peer(k), g), (x_peer(k), g), (d, twin)][n]
        return pltpu.make_async_remote_copy(
            ref, ref, pss.at[n, k], prs.at[n, k], device_id=to, device_id_type=MESH
        )

    def weights_from(n, k):
        ref = [
            wall.at[core, xd, lax.rem(zd + 4 - k, 4)],
            wall.at[core, lax.rem(xd + 4 - k, 4)],
            wall.at[1 - core],
        ][n]
        return pltpu.make_async_remote_copy(
            ref, ref, pss.at[n, k], prs.at[n, k], device_id=(d, twin), device_id_type=MESH
        )

    def weights_start(n):
        for k in range(1, 4 if n < 2 else 2):
            weights_copy(n, k).start()

    def weights_wait(n):
        for k in range(1, 4 if n < 2 else 2):
            weights_from(n, k).wait()

    def slab_copies(n, ts):
        mid = pl.ds(ROWS, ROWS)
        for i, (src, dst, dd) in enumerate([(1, CD + 1, down), (CD, 0, up)]):
            yield pltpu.make_async_remote_copy(
                ts.at[src, mid, :], ts.at[dst, mid, :], hss.at[n, i], hrs.at[n, i], device_id=(dd, g), device_id_type=MESH
            )

    def edge_copies(n):
        i = 2
        for side, gg in ((0, left), (1, right)):
            base = 64 * (1 - side)
            for src, rows, dst, dd in ((0, 32, 0, d), (16, 16, 32, up), (0, 16, 48, down)):
                yield pltpu.make_async_remote_copy(
                    eb.at[n, pl.ds(32 * side + src, rows), :],
                    rx.at[n, pl.ds(base + dst, rows), :],
                    hss.at[n, i],
                    hrs.at[n, i],
                    device_id=(dd, gg),
                    device_id_type=MESH,
                )
                i += 1


    def wait_vol(z, _):
        vol_load(z).wait()
        return 0

    lax.fori_loop(0, CD, wait_vol, 0)
    flat = vol.reshape(CD, ROWS, LANES)
    erow = iota((64, LANES), 0)
    elane = iota((64, LANES), 1)

    def edges_of(z, slab):
        pick = ((erow == z) & (elane == 0)) | ((erow == z + 32) & (elane == LANES - 1))
        return dot(one_hot(pick), slab, 1, 1)

    def edge_step(z, edge):
        return edge + edges_of(z, flat[z])

    eb[0] = lax.fori_loop(0, CD, edge_step, jnp.zeros((64, LANES), F32), unroll=12).astype(BF16)
    vs[1, ROWS : 2 * ROWS, :] = flat[0]
    vs[CD, ROWS : 2 * ROWS, :] = flat[CD - 1]
    loads[1].wait()


    def compress(i, _):
        r0 = pl.multiple_of(i * 32, 32)
        both = [flat[:, pl.ds(r0 + 16 * j, 16), :].reshape(CD * 16, LANES) for j in range(2)]
        res = dot(hk[...], jnp.concatenate(both, axis=1)).astype(BF16)
        for j in range(2):
            gb[:, pl.ds(r0 + 16 * j, 16), :] = res[:, LANES * j : LANES * (j + 1)].reshape(R, 16, LANES)
        return 0

    lax.fori_loop(0, ROWS // 32, compress, 0, unroll=4)

    for p in range(R // 2):
        pair = [dot(gb[2 * p + j], perm, 0, 0).reshape(ND, XO, LANES) for j in range(2)]
        fs[:, 16 * p : 16 * p + 16, :] = jnp.concatenate(pair, axis=1).astype(BF16)
    fr[d] = fs[d]


    def spectral_copy(src, dst, send, recv, t):
        return pltpu.make_async_remote_copy(
            src.at[t], dst.at[d], send.at[t], recv.at[d], device_id=(t, g), device_id_type=MESH
        )

    def spectral_from(src, dst, send, recv, t):
        return pltpu.make_async_remote_copy(
            src.at[t], dst.at[t], send.at[t], recv.at[t], device_id=(t, g), device_id_type=MESH
        )

    pl.semaphore_wait(barrier, ND - 1 + 1 + 2 + 4)
    weights_start(0)
    for c in edge_copies(0):
        c.start()
    for c in slab_copies(0, vs):
        c.start()

    def send_forward(j, _):
        spectral_copy(fs, fr, fss, frs, far_first(j)).start()
        return 0

    lax.fori_loop(0, ND - 1, send_forward, 0)

    def spread(ts, zi, slab):
        ts[zi, 0:ROWS, :] = pltpu.roll(slab, 1, 1)
        ts[zi, ROWS : 2 * ROWS, :] = slab
        ts[zi, 2 * ROWS : 3 * ROWS, :] = pltpu.roll(slab, LANES - 1, 1)

    def fill(z, _):
        spread(vs, z + 1, flat[z])
        return 0

    for z in (0, CD - 1):
        slab = flat[z]
        vs[z + 1, 0:ROWS, :] = pltpu.roll(slab, 1, 1)
        vs[z + 1, 2 * ROWS : 3 * ROWS, :] = pltpu.roll(slab, LANES - 1, 1)
    lax.fori_loop(1, CD - 1, fill, 0, unroll=11)
    loads[2].wait()
    loads[4].wait()

    def taps(t, _):
        a, e = t // 3, lax.rem(t, 3)

        def halves(w):
            w0, w1, w2 = w[a, 0, e], w[a, 1, e], w[a, 2, e]
            return jnp.concatenate([w1, w0], axis=0), jnp.concatenate([w2, w1], axis=0)

        lo, hi = halves(wc1)
        wa[t] = (dot(lo, permt[:C]) + dot(hi, permt[C:])).astype(BF16)
        lo, hi = halves(wc2)
        both = (dot(lo, eye[:C]) + dot(hi, eye[C:])).astype(BF16)
        wb[t] = dot(perm, both).astype(BF16)
        return 0

    lax.fori_loop(0, 9, taps, 0, unroll=3)


    def complete(n, ts):
        for c in slab_copies(n, ts):
            c.wait()
        for c in edge_copies(n):
            c.wait()
        for zi, there in ((0, d > 0), (CD + 1, d < ND - 1)):
            slab = ts[zi, ROWS : 2 * ROWS, :].astype(F32) * jnp.where(there, 1.0, 0.0)
            spread(ts, zi, slab.astype(BF16))
        sub = row & 63
        inside = jnp.where(row < 64, g, NG - 1 - g)
        slabs = jnp.where(sub < 32, 1, jnp.where(sub < 48, d, ND - 1 - d))
        keep = jnp.minimum(inside, slabs) > 0
        cells = jnp.where(keep, rx[n].astype(F32), 0.0).astype(BF16)
        columns = dot(eye, cells, 1, 1).astype(BF16)
        wrow = iota((ROWS, 2 * LANES), 0)
        wlane = iota((ROWS, 2 * LANES), 1)

        def patch(zi, _):
            rho = jnp.where(zi == 0, 39, jnp.where(zi == CD + 1, 48, zi - 1))
            put = ((wrow == rho) & (wlane == 0)) | ((wrow == rho + 64) & (wlane == 2 * LANES - 1))
            ins = dot(columns, one_hot(put)).astype(BF16)
            ts[zi, 0:ROWS, :] = jnp.where(lane == 0, ins[:, :LANES], ts[zi, 0:ROWS, :])
            ts[zi, 2 * ROWS : 3 * ROWS, :] = jnp.where(
                lane == LANES - 1, ins[:, LANES:], ts[zi, 2 * ROWS : 3 * ROWS, :]
            )
            return 0

        lax.fori_loop(0, CD + 2, patch, 0, unroll=13)

    def conv_pair(w, ts, z):
        lhs = jnp.concatenate([w[t] for t in range(9)], axis=1)
        rhs = [ts[pl.ds(z + j, 3)].reshape(9 * ROWS, LANES) for j in range(2)]
        return dot(lhs, jnp.concatenate(rhs, axis=1))

    weights_wait(0)
    weights_start(1)
    complete(0, vs)
    weights_wait(1)
    weights_start(2)

    def first(i, edge):
        z = 2 * i
        hidden = gelu(conv_pair(wa, vs, z)).astype(BF16)
        for j in range(2):
            slab = hidden[:, LANES * j : LANES * (j + 1)]
            spread(hs, z + j + 1, slab)
            edge = edge + edges_of(z + j, slab)
        return edge

    eb[1] = lax.fori_loop(0, CD // 2, first, jnp.zeros((64, LANES), F32), unroll=2).astype(BF16)
    for c in slab_copies(1, hs):
        c.start()
    for c in edge_copies(1):
        c.start()

    half = iota((C, LANES), 1) < C

    def diagonal(p):
        def step(owner, _):
            i = 2 * owner + p
            w = wall[p, owner // 4, lax.rem(owner, 4)].astype(F32)
            turned = pltpu.roll(w, C, 1)
            top = [jnp.where(half, w, 0.0), jnp.where(half, turned, 0.0)]
            bottom = [jnp.where(half, 0.0, turned), jnp.where(half, 0.0, w)]
            bd[i, 0:C, :] = jnp.concatenate(top, axis=1).astype(BF16)
            bd[i, C : 2 * C, :] = jnp.concatenate(bottom, axis=1).astype(BF16)
            return 0

        return step

    lax.fori_loop(0, ND, diagonal(core), 0, unroll=4)
    weights_wait(2)
    lax.fori_loop(0, ND, diagonal(1 - core), 0, unroll=4)

    loads[3].wait()
    loads[5].wait()

    def wait_forward(k, _):
        spectral_from(fs, fr, fss, frs, depth_peer(k)).wait()
        return 0

    lax.fori_loop(1, ND, wait_forward, 0)
    coef[...] = dot(gk[...], fr[...].reshape(ND * R * XO, LANES)).astype(BF16)

    def mix(i, _):
        rows = pl.ds(pl.multiple_of(16 * i, 16), 16)
        res = dot(coef[rows, :], bd[i])
        mixed[rows, :] = jnp.concatenate([res[:8, :LANES], res[8:, LANES:]], axis=0).astype(BF16)
        return 0

    lax.fori_loop(0, M // 2, mix, 0, unroll=8)
    def send_back(xs, count):
        n = 4 * R * XO
        rows = pl.ds(pl.multiple_of(xs * n, 16), n)
        bs[pl.ds(xs * 4, 4)] = dot(gkt[rows, :], mixed[...]).astype(BF16).reshape(4, R * XO, LANES)

        def step(j, _):
            far = half_z + (1 - j // 2) * (1 - 2 * half_z)
            spectral_copy(bs, br, bss, brs, xs * 4 + 2 * far + lax.rem(zd + j + 1, 2)).start()
            return 0

        lax.fori_loop(0, count, step, 0)

    for k in (2, 1, 3):
        send_back(lax.rem(xd + k, 4), 4)
    send_back(xd, 3)
    br[d] = bs[d]

    complete(1, hs)

    def second(i, _):
        z = 2 * i
        res = conv_pair(wb, hs, z)
        for j in range(2):
            acc[z + j] = flat[z + j].astype(F32) + res[:, LANES * j : LANES * (j + 1)]
        return 0

    lax.fori_loop(0, CD // 2, second, 0, unroll=2)

    loads[6].wait()

    def wait_back(k, _):
        spectral_from(bs, br, bss, brs, depth_peer(k)).wait()
        return 0

    lax.fori_loop(1, ND, wait_back, 0)
    for p in range(R // 2):
        pair = br[:, 16 * p : 16 * p + 16, :].astype(F32)
        for j in range(2):
            cols = pair[:, XO * j : XO * (j + 1)].reshape(LANES, ROWS).astype(BF16)
            gb[2 * p + j] = dot(perm, cols, 1, 1).astype(BF16)

    def expand(i, _):
        r0 = pl.multiple_of(i * 32, 32)
        both = [gb[:, pl.ds(r0 + 16 * j, 16), :].reshape(R * 16, LANES) for j in range(2)]
        res = dot(hkt[...], jnp.concatenate(both, axis=1))
        for j in range(2):
            rows = pl.ds(r0 + 16 * j, 16)
            total = acc[:, rows, :] + res[:, LANES * j : LANES * (j + 1)].reshape(CD, 16, LANES)
            res_out[:, rows, :] = total.astype(BF16)
            put_out(i, j).start()
        return 0

    def put_out(i, j):
        rows = pl.ds(pl.multiple_of(i * 32, 32) + 16 * j, 16)
        return pltpu.make_async_copy(res_out.at[:, rows, :], out.at[:, rows, :], out_sem.at[2 * i + j])

    lax.fori_loop(0, ROWS // 32, expand, 0, unroll=4)
    for i in range(ROWS // 32):
        for j in range(2):
            put_out(i, j).wait()


def local(volume, conv_first, conv_second, mode_weights):
    vmem = pltpu.VMEM
    dma = pltpu.SemaphoreType.DMA
    hbm = pl.BlockSpec(memory_space=pltpu.HBM)
    res = pl.pallas_call(
        kernel,
        out_shape=jax.ShapeDtypeStruct((CD, ROWS, LANES), BF16),
        in_specs=[hbm] * 8,
        out_specs=pl.BlockSpec(memory_space=pltpu.HBM),
        scratch_shapes=[
            vmem((CD, C, 2, LANES), BF16),
            vmem((3, 3, 3, C, C), BF16),
            vmem((3, 3, 3, C, C), BF16),
            vmem((4, C, C), BF16),
            vmem((R * 16, CD * 16), BF16),
            vmem((CD * 16, R * 16), BF16),
            vmem((M * XO, ND * R * XO), BF16),
            vmem((ND * R * XO, M * XO), BF16),
            vmem((CD + 2, 3 * ROWS, LANES), BF16),
            vmem((CD + 2, 3 * ROWS, LANES), BF16),
            vmem((9, ROWS, LANES), BF16),
            vmem((9, ROWS, LANES), BF16),
            vmem((CD, ROWS, LANES), F32),
            vmem((2, 64, LANES), BF16),
            vmem((2, ROWS, LANES), BF16),
            vmem((R, ROWS, LANES), BF16),
            vmem((ND, R * XO, LANES), BF16),
            vmem((ND, R * XO, LANES), BF16),
            vmem((ND, R * XO, LANES), BF16),
            vmem((ND, R * XO, LANES), BF16),
            vmem((M * XO, LANES), BF16),
            vmem((M * XO, LANES), BF16),
            vmem((2, 4, 4, C, LANES), BF16),
            vmem((M // 2, ROWS, 2 * LANES), BF16),
            vmem((CD, ROWS, LANES), BF16),
            dma((7,)),
            dma((CD,)),
            dma((ND,)),
            dma((ND,)),
            dma((ND,)),
            dma((ND,)),
            dma((3, 4)),
            dma((3, 4)),
            dma((2, 8)),
            dma((2, 8)),
            dma((8,)),
        ],
        compiler_params=pltpu.CompilerParams(
            collective_id=0, has_side_effects=True, vmem_limit_bytes=60 * 2**20
        ),
    )(volume, conv_first, conv_second, mode_weights, *constants())
    return res.reshape(CD, C, 2, LANES).transpose(1, 0, 2, 3)


def solution(mesh):
    placed = (P(None, "depth", None, "gx"), P(), P(), P("depth", None, None))
    return jax.shard_map(
        local, mesh=mesh, in_specs=placed, out_specs=P(None, "depth", None, "gx"), check_vma=False
    )
```

```python
import math

import jax
import jax.numpy as jnp
import ml_dtypes
import numpy as np
from jax import lax
from jax.experimental import pallas as pl
from jax.experimental.pallas import tpu as pltpu
from jax.sharding import PartitionSpec as P

MODES = 32
M = 2 * MODES
C = 64
ROWS = 128
LANES = 128
CD = 24
NZ = 384
ND = 16
NG = 16
R = 10
XO = LANES // ND
MESH = pl.DeviceIdType.MESH
F32 = jnp.float32
BF16 = jnp.bfloat16


def slab_factors():
    mode = np.arange(M)
    k = np.where(mode < MODES, mode, mode - MODES + 1)
    t = k[:, None] * (2 * np.arange(NZ)[None, :] + 1) * (math.pi / (2 * NZ))
    basis = math.sqrt(2.0 / NZ) * np.where((mode < MODES)[:, None], np.cos(t), np.sin(t))
    z = np.arange(CD) - (CD - 1) / 2
    a = np.arange(MODES + 1)[:, None] * z[None, :] * (math.pi / NZ)
    h = np.linalg.svd(np.concatenate([np.cos(a), np.sin(a)]))[2][:R]
    g = np.einsum("msz,rz->msr", basis.reshape(M, ND, CD), h)
    return g.reshape(M, ND * R), h


def constants():
    g, h = slab_factors()
    hk = np.kron(h, np.eye(16)).astype(ml_dtypes.bfloat16)
    gk = np.kron(g, np.eye(XO)).astype(ml_dtypes.bfloat16)
    return hk, np.ascontiguousarray(hk.T), gk, np.ascontiguousarray(gk.T)


def dot(a, b, ca=1, cb=0):
    return lax.dot_general(a, b, (((ca,), (cb,)), ((), ())), preferred_element_type=F32)


def iota(shape, dim):
    return lax.broadcasted_iota(jnp.int32, shape, dim)


def one_hot(mask):
    return jnp.where(mask, 1.0, 0.0).astype(BF16)


def gelu(x):
    inner = math.sqrt(2.0 / math.pi) * (x + 0.044715 * (x * x * x))
    return 0.5 * x * (1.0 + jnp.tanh(inner))


def kernel(
    vol_h, w1_h, w2_h, mw_h, hk_h, hkt_h, gk_h, gkt_h, out,
    vol, wc1, wc2, mw, hk, hkt, gk, gkt,
    vs, hs, wa, wb, acc, eb, rx,
    gb, fs, fr, bs, br, coef, mixed,
    wall, bd, res_out,
    load_sem, vol_sem, fss, frs, bss, brs, pss, prs, hss, hrs, out_sem,
):
    d = lax.axis_index("depth")
    g = lax.axis_index("gx")
    xd, zd = d // 4, lax.rem(d, 4)
    core = lax.rem(g, 2)
    half_z = zd // 2

    def depth_peer(k):
        return lax.rem(d + k, ND)

    def z_peer(k):
        return xd * 4 + lax.rem(zd + k, 4)

    def x_peer(k):
        return lax.rem(xd + k, 4) * 4 + zd

    def far_first(j):
        other = 1 - j // 8
        z = 2 * (half_z + other * (1 - 2 * half_z)) + lax.rem(zd + j + 1, 2)
        return lax.rem(xd + 1 + lax.rem(j, 8) // 2, 4) * 4 + z

    loads = [
        pltpu.make_async_copy(s, t, load_sem.at[i])
        for i, (s, t) in enumerate(
            [(mw_h, mw), (hk_h, hk), (w1_h, wc1), (gk_h, gk), (w2_h, wc2), (gkt_h, gkt), (hkt_h, hkt)]
        )
    ]

    def vol_load(z):
        return pltpu.make_async_copy(vol_h.at[:, z], vol.at[z], vol_sem.at[z])

    loads[0].start()
    loads[1].start()

    def start_vol(z, _):
        vol_load(z).start()
        return 0

    lax.fori_loop(0, CD, start_vol, 0)
    for c in loads[2:]:
        c.start()

    barrier = pltpu.get_barrier_semaphore()

    def greet(dd, gg):
        pl.semaphore_signal(barrier, 1, device_id=(dd, gg), device_id_type=MESH)

    def greet_depth(k, _):
        greet(depth_peer(k), g)
        return 0

    lax.fori_loop(1, ND, greet_depth, 0)

    twin = g + 1 - 2 * core
    for k in range(4):
        greet(x_peer(k), twin)
    up, down = lax.rem(d + 1, ND), lax.rem(d + ND - 1, ND)
    right, left = lax.rem(g + 1, NG), lax.rem(g + NG - 1, NG)
    greet(d, right)
    greet(d, left)
    for dd in (up, down):
        for gg in (right, left):
            greet(dd, gg)

    row = iota((ROWS, LANES), 0)
    lane = iota((ROWS, LANES), 1)
    eye = one_hot(row == lane)
    perm = one_hot(lane == (row & 1) * C + (row >> 1))
    permt = one_hot(row == (lane & 1) * C + (lane >> 1))

    loads[0].wait()
    two = mw[pl.ds(2 * core, 2)].reshape(2 * C, C)
    wall[core, xd, zd] = dot(eye[:C, :C], two, 1, 1).astype(BF16)

    def weights_copy(n, k):
        ref = wall.at[core, xd, zd] if n == 0 else wall.at[core, xd]
        to = (z_peer(k), g) if n == 0 else (x_peer(k % 4), g if k < 4 else twin)
        return pltpu.make_async_remote_copy(
            ref, ref, pss.at[n, k], prs.at[n, k], device_id=to, device_id_type=MESH
        )

    def weights_from(n, k):
        if n == 0:
            ref = wall.at[core, xd, lax.rem(zd + 4 - k, 4)]
        else:
            ref = wall.at[core if k < 4 else 1 - core, lax.rem(xd + 8 - k, 4)]
        return pltpu.make_async_remote_copy(
            ref, ref, pss.at[n, k], prs.at[n, k], device_id=(d, twin), device_id_type=MESH
        )

    def weights_start(n):
        for k in range(1, 4 + 4 * n):
            weights_copy(n, k).start()

    def weights_wait(n):
        for k in range(1, 4 + 4 * n):
            weights_from(n, k).wait()

    def slab_copies(n, ts):
        mid = pl.ds(ROWS, ROWS)
        for i, (src, dst, dd) in enumerate([(1, CD + 1, down), (CD, 0, up)]):
            yield pltpu.make_async_remote_copy(
                ts.at[src, mid, :], ts.at[dst, mid, :], hss.at[n, i], hrs.at[n, i], device_id=(dd, g), device_id_type=MESH
            )

    def edge_copies(n):
        i = 2
        for side, gg in ((0, left), (1, right)):
            base = 64 * (1 - side)
            for src, rows, dst, dd in ((0, 32, 0, d), (16, 16, 32, up), (0, 16, 48, down)):
                yield pltpu.make_async_remote_copy(
                    eb.at[n, pl.ds(32 * side + src, rows), :],
                    rx.at[n, pl.ds(base + dst, rows), :],
                    hss.at[n, i],
                    hrs.at[n, i],
                    device_id=(dd, gg),
                    device_id_type=MESH,
                )
                i += 1


    def wait_vol(z, _):
        vol_load(z).wait()
        return 0

    lax.fori_loop(0, CD, wait_vol, 0)
    flat = vol.reshape(CD, ROWS, LANES)
    erow = iota((64, LANES), 0)
    elane = iota((64, LANES), 1)

    def edges_of(z, slab):
        pick = ((erow == z) & (elane == 0)) | ((erow == z + 32) & (elane == LANES - 1))
        return dot(one_hot(pick), slab, 1, 1)

    def edge_step(z, edge):
        return edge + edges_of(z, flat[z])

    eb[0] = lax.fori_loop(0, CD, edge_step, jnp.zeros((64, LANES), F32), unroll=12).astype(BF16)
    vs[1, ROWS : 2 * ROWS, :] = flat[0]
    vs[CD, ROWS : 2 * ROWS, :] = flat[CD - 1]
    loads[1].wait()


    def compress(i, _):
        r0 = pl.multiple_of(i * 32, 32)
        both = [flat[:, pl.ds(r0 + 16 * j, 16), :].reshape(CD * 16, LANES) for j in range(2)]
        res = dot(hk[...], jnp.concatenate(both, axis=1)).astype(BF16)
        for j in range(2):
            gb[:, pl.ds(r0 + 16 * j, 16), :] = res[:, LANES * j : LANES * (j + 1)].reshape(R, 16, LANES)
        return 0

    lax.fori_loop(0, ROWS // 32, compress, 0, unroll=4)

    for p in range(R // 2):
        pair = [dot(gb[2 * p + j], perm, 0, 0).reshape(ND, XO, LANES) for j in range(2)]
        fs[:, 16 * p : 16 * p + 16, :] = jnp.concatenate(pair, axis=1).astype(BF16)
    fr[d] = fs[d]


    def spectral_copy(src, dst, send, recv, t):
        return pltpu.make_async_remote_copy(
            src.at[t], dst.at[d], send.at[t], recv.at[d], device_id=(t, g), device_id_type=MESH
        )

    def spectral_from(src, dst, send, recv, t):
        return pltpu.make_async_remote_copy(
            src.at[t], dst.at[t], send.at[t], recv.at[t], device_id=(t, g), device_id_type=MESH
        )

    pl.semaphore_wait(barrier, ND - 1 + 4 + 2 + 4)
    weights_start(0)
    for c in edge_copies(0):
        c.start()
    for c in slab_copies(0, vs):
        c.start()

    def send_forward(j, _):
        spectral_copy(fs, fr, fss, frs, far_first(j)).start()
        return 0

    lax.fori_loop(0, ND - 1, send_forward, 0)

    def spread(ts, zi, slab):
        ts[zi, 0:ROWS, :] = pltpu.roll(slab, 1, 1)
        ts[zi, ROWS : 2 * ROWS, :] = slab
        ts[zi, 2 * ROWS : 3 * ROWS, :] = pltpu.roll(slab, LANES - 1, 1)

    def fill(z, _):
        spread(vs, z + 1, flat[z])
        return 0

    for z in (0, CD - 1):
        slab = flat[z]
        vs[z + 1, 0:ROWS, :] = pltpu.roll(slab, 1, 1)
        vs[z + 1, 2 * ROWS : 3 * ROWS, :] = pltpu.roll(slab, LANES - 1, 1)
    lax.fori_loop(1, CD - 1, fill, 0, unroll=11)
    loads[2].wait()
    loads[4].wait()

    def taps(t, _):
        a, e = t // 3, lax.rem(t, 3)

        def halves(w):
            w0, w1, w2 = w[a, 0, e], w[a, 1, e], w[a, 2, e]
            return jnp.concatenate([w1, w0], axis=0), jnp.concatenate([w2, w1], axis=0)

        lo, hi = halves(wc1)
        wa[t] = (dot(lo, permt[:C]) + dot(hi, permt[C:])).astype(BF16)
        lo, hi = halves(wc2)
        both = (dot(lo, eye[:C]) + dot(hi, eye[C:])).astype(BF16)
        wb[t] = dot(perm, both).astype(BF16)
        return 0

    lax.fori_loop(0, 9, taps, 0, unroll=3)


    def complete(n, ts):
        for c in slab_copies(n, ts):
            c.wait()
        for c in edge_copies(n):
            c.wait()
        for zi, there in ((0, d > 0), (CD + 1, d < ND - 1)):
            slab = ts[zi, ROWS : 2 * ROWS, :].astype(F32) * jnp.where(there, 1.0, 0.0)
            spread(ts, zi, slab.astype(BF16))
        sub = row & 63
        inside = jnp.where(row < 64, g, NG - 1 - g)
        slabs = jnp.where(sub < 32, 1, jnp.where(sub < 48, d, ND - 1 - d))
        keep = jnp.minimum(inside, slabs) > 0
        cells = jnp.where(keep, rx[n].astype(F32), 0.0).astype(BF16)
        columns = dot(eye, cells, 1, 1).astype(BF16)
        wrow = iota((ROWS, 2 * LANES), 0)
        wlane = iota((ROWS, 2 * LANES), 1)

        def patch(zi, _):
            rho = jnp.where(zi == 0, 39, jnp.where(zi == CD + 1, 48, zi - 1))
            put = ((wrow == rho) & (wlane == 0)) | ((wrow == rho + 64) & (wlane == 2 * LANES - 1))
            ins = dot(columns, one_hot(put)).astype(BF16)
            ts[zi, 0:ROWS, :] = jnp.where(lane == 0, ins[:, :LANES], ts[zi, 0:ROWS, :])
            ts[zi, 2 * ROWS : 3 * ROWS, :] = jnp.where(
                lane == LANES - 1, ins[:, LANES:], ts[zi, 2 * ROWS : 3 * ROWS, :]
            )
            return 0

        lax.fori_loop(0, CD + 2, patch, 0, unroll=13)

    def conv_pair(w, ts, z):
        lhs = jnp.concatenate([w[t] for t in range(9)], axis=1)
        rhs = [ts[pl.ds(z + j, 3)].reshape(9 * ROWS, LANES) for j in range(2)]
        return dot(lhs, jnp.concatenate(rhs, axis=1))

    weights_wait(0)
    weights_start(1)
    complete(0, vs)

    def first(i, edge):
        z = 2 * i
        hidden = gelu(conv_pair(wa, vs, z)).astype(BF16)
        for j in range(2):
            slab = hidden[:, LANES * j : LANES * (j + 1)]
            spread(hs, z + j + 1, slab)
            edge = edge + edges_of(z + j, slab)
        return edge

    eb[1] = lax.fori_loop(0, CD // 2, first, jnp.zeros((64, LANES), F32), unroll=2).astype(BF16)
    for c in slab_copies(1, hs):
        c.start()
    for c in edge_copies(1):
        c.start()

    half = iota((C, LANES), 1) < C

    def diagonal(i, _):
        owner = i // 2
        w = wall[lax.rem(i, 2), owner // 4, lax.rem(owner, 4)].astype(F32)
        turned = pltpu.roll(w, C, 1)
        top = [jnp.where(half, w, 0.0), jnp.where(half, turned, 0.0)]
        bottom = [jnp.where(half, 0.0, turned), jnp.where(half, 0.0, w)]
        bd[i, 0:C, :] = jnp.concatenate(top, axis=1).astype(BF16)
        bd[i, C : 2 * C, :] = jnp.concatenate(bottom, axis=1).astype(BF16)
        return 0

    weights_wait(1)
    lax.fori_loop(0, M // 2, diagonal, 0, unroll=4)

    loads[3].wait()
    loads[5].wait()

    def wait_forward(k, _):
        spectral_from(fs, fr, fss, frs, depth_peer(k)).wait()
        return 0

    lax.fori_loop(1, ND, wait_forward, 0)
    coef[...] = dot(gk[...], fr[...].reshape(ND * R * XO, LANES)).astype(BF16)

    def mix(i, _):
        rows = pl.ds(pl.multiple_of(16 * i, 16), 16)
        res = dot(coef[rows, :], bd[i])
        mixed[rows, :] = jnp.concatenate([res[:8, :LANES], res[8:, LANES:]], axis=0).astype(BF16)
        return 0

    lax.fori_loop(0, M // 2, mix, 0, unroll=8)
    def send_back(xs, count):
        n = 4 * R * XO
        rows = pl.ds(pl.multiple_of(xs * n, 16), n)
        bs[pl.ds(xs * 4, 4)] = dot(gkt[rows, :], mixed[...]).astype(BF16).reshape(4, R * XO, LANES)

        def step(j, _):
            far = half_z + (1 - j // 2) * (1 - 2 * half_z)
            spectral_copy(bs, br, bss, brs, xs * 4 + 2 * far + lax.rem(zd + j + 1, 2)).start()
            return 0

        lax.fori_loop(0, count, step, 0)

    for k in (2, 1, 3):
        send_back(lax.rem(xd + k, 4), 4)
    send_back(xd, 3)
    br[d] = bs[d]

    complete(1, hs)

    def second(i, _):
        z = 2 * i
        res = conv_pair(wb, hs, z)
        for j in range(2):
            acc[z + j] = flat[z + j].astype(F32) + res[:, LANES * j : LANES * (j + 1)]
        return 0

    lax.fori_loop(0, CD // 2, second, 0, unroll=2)

    loads[6].wait()

    def wait_back(k, _):
        spectral_from(bs, br, bss, brs, depth_peer(k)).wait()
        return 0

    lax.fori_loop(1, ND, wait_back, 0)
    for p in range(R // 2):
        pair = br[:, 16 * p : 16 * p + 16, :].astype(F32)
        for j in range(2):
            cols = pair[:, XO * j : XO * (j + 1)].reshape(LANES, ROWS).astype(BF16)
            gb[2 * p + j] = dot(perm, cols, 1, 1).astype(BF16)

    def expand(i, _):
        r0 = pl.multiple_of(i * 32, 32)
        both = [gb[:, pl.ds(r0 + 16 * j, 16), :].reshape(R * 16, LANES) for j in range(2)]
        res = dot(hkt[...], jnp.concatenate(both, axis=1))
        for j in range(2):
            rows = pl.ds(r0 + 16 * j, 16)
            total = acc[:, rows, :] + res[:, LANES * j : LANES * (j + 1)].reshape(CD, 16, LANES)
            res_out[:, rows, :] = total.astype(BF16)
            put_out(i, j).start()
        return 0

    def put_out(i, j):
        rows = pl.ds(pl.multiple_of(i * 32, 32) + 16 * j, 16)
        return pltpu.make_async_copy(res_out.at[:, rows, :], out.at[:, rows, :], out_sem.at[2 * i + j])

    lax.fori_loop(0, ROWS // 32, expand, 0, unroll=4)
    for i in range(ROWS // 32):
        for j in range(2):
            put_out(i, j).wait()


def local(volume, conv_first, conv_second, mode_weights):
    vmem = pltpu.VMEM
    dma = pltpu.SemaphoreType.DMA
    hbm = pl.BlockSpec(memory_space=pltpu.HBM)
    res = pl.pallas_call(
        kernel,
        out_shape=jax.ShapeDtypeStruct((CD, ROWS, LANES), BF16),
        in_specs=[hbm] * 8,
        out_specs=pl.BlockSpec(memory_space=pltpu.HBM),
        scratch_shapes=[
            vmem((CD, C, 2, LANES), BF16),
            vmem((3, 3, 3, C, C), BF16),
            vmem((3, 3, 3, C, C), BF16),
            vmem((4, C, C), BF16),
            vmem((R * 16, CD * 16), BF16),
            vmem((CD * 16, R * 16), BF16),
            vmem((M * XO, ND * R * XO), BF16),
            vmem((ND * R * XO, M * XO), BF16),
            vmem((CD + 2, 3 * ROWS, LANES), BF16),
            vmem((CD + 2, 3 * ROWS, LANES), BF16),
            vmem((9, ROWS, LANES), BF16),
            vmem((9, ROWS, LANES), BF16),
            vmem((CD, ROWS, LANES), F32),
            vmem((2, 64, LANES), BF16),
            vmem((2, ROWS, LANES), BF16),
            vmem((R, ROWS, LANES), BF16),
            vmem((ND, R * XO, LANES), BF16),
            vmem((ND, R * XO, LANES), BF16),
            vmem((ND, R * XO, LANES), BF16),
            vmem((ND, R * XO, LANES), BF16),
            vmem((M * XO, LANES), BF16),
            vmem((M * XO, LANES), BF16),
            vmem((2, 4, 4, C, LANES), BF16),
            vmem((M // 2, ROWS, 2 * LANES), BF16),
            vmem((CD, ROWS, LANES), BF16),
            dma((7,)),
            dma((CD,)),
            dma((ND,)),
            dma((ND,)),
            dma((ND,)),
            dma((ND,)),
            dma((2, 8)),
            dma((2, 8)),
            dma((2, 8)),
            dma((2, 8)),
            dma((8,)),
        ],
        compiler_params=pltpu.CompilerParams(
            collective_id=0, has_side_effects=True, vmem_limit_bytes=60 * 2**20
        ),
    )(volume, conv_first, conv_second, mode_weights, *constants())
    return res.reshape(CD, C, 2, LANES).transpose(1, 0, 2, 3)


def solution(mesh):
    placed = (P(None, "depth", None, "gx"), P(), P(), P("depth", None, None))
    return jax.shard_map(
        local, mesh=mesh, in_specs=placed, out_specs=P(None, "depth", None, "gx"), check_vma=False
    )
```

```python
import math

import jax
import jax.numpy as jnp
import ml_dtypes
import numpy as np
from jax import lax
from jax.experimental import pallas as pl
from jax.experimental.pallas import tpu as pltpu
from jax.sharding import PartitionSpec as P

MODES = 32
M = 2 * MODES
C = 64
ROWS = 128
LANES = 128
CD = 24
NZ = 384
ND = 16
NG = 16
R = 10
XO = LANES // ND
MESH = pl.DeviceIdType.MESH
F32 = jnp.float32
BF16 = jnp.bfloat16


def slab_factors():
    mode = np.arange(M)
    k = np.where(mode < MODES, mode, mode - MODES + 1)
    t = k[:, None] * (2 * np.arange(NZ)[None, :] + 1) * (math.pi / (2 * NZ))
    basis = math.sqrt(2.0 / NZ) * np.where((mode < MODES)[:, None], np.cos(t), np.sin(t))
    z = np.arange(CD) - (CD - 1) / 2
    a = np.arange(MODES + 1)[:, None] * z[None, :] * (math.pi / NZ)
    h = np.linalg.svd(np.concatenate([np.cos(a), np.sin(a)]))[2][:R]
    g = np.einsum("msz,rz->msr", basis.reshape(M, ND, CD), h)
    return g.reshape(M, ND * R), h


def constants():
    g, h = slab_factors()
    hk = np.kron(h, np.eye(16)).astype(ml_dtypes.bfloat16)
    gk = np.kron(g, np.eye(XO)).astype(ml_dtypes.bfloat16)
    return hk, np.ascontiguousarray(hk.T), gk, np.ascontiguousarray(gk.T)


def dot(a, b, ca=1, cb=0):
    return lax.dot_general(a, b, (((ca,), (cb,)), ((), ())), preferred_element_type=F32)


def iota(shape, dim):
    return lax.broadcasted_iota(jnp.int32, shape, dim)


def one_hot(mask):
    return jnp.where(mask, 1.0, 0.0).astype(BF16)


def gelu(x):
    inner = math.sqrt(2.0 / math.pi) * (x + 0.044715 * (x * x * x))
    return 0.5 * x * (1.0 + jnp.tanh(inner))


def kernel(
    vol_h, w1_h, w2_h, mw_h, hk_h, hkt_h, gk_h, gkt_h, out,
    vol, wc1, wc2, mw, hk, hkt, gk, gkt,
    vs, hs, wa, wb, acc, eb, rx,
    gb, fs, fr, bs, br, coef, mixed,
    wall, bd, res_out,
    load_sem, vol_sem, fss, frs, bss, brs, pss, prs, hss, hrs, out_sem,
):
    d = lax.axis_index("depth")
    g = lax.axis_index("gx")
    xd, zd = d // 4, lax.rem(d, 4)
    core = lax.rem(g, 2)
    half_z = zd // 2

    def depth_peer(k):
        return lax.rem(d + k, ND)

    def z_peer(k):
        return xd * 4 + lax.rem(zd + k, 4)

    def x_peer(k):
        return lax.rem(xd + k, 4) * 4 + zd

    def far_first(j):
        other = 1 - j // 8
        z = 2 * (half_z + other * (1 - 2 * half_z)) + lax.rem(zd + j + 1, 2)
        return lax.rem(xd + 1 + lax.rem(j, 8) // 2, 4) * 4 + z

    loads = [
        pltpu.make_async_copy(s, t, load_sem.at[i])
        for i, (s, t) in enumerate(
            [(mw_h, mw), (hk_h, hk), (w1_h, wc1), (gk_h, gk), (w2_h, wc2), (gkt_h, gkt), (hkt_h, hkt)]
        )
    ]

    def vol_load(z):
        return pltpu.make_async_copy(vol_h.at[:, z], vol.at[z], vol_sem.at[z])

    loads[0].start()
    loads[1].start()

    def start_vol(z, _):
        vol_load(z).start()
        return 0

    lax.fori_loop(0, CD, start_vol, 0)
    for c in loads[2:]:
        c.start()

    barrier = pltpu.get_barrier_semaphore()

    def greet(dd, gg):
        pl.semaphore_signal(barrier, 1, device_id=(dd, gg), device_id_type=MESH)

    def greet_depth(k, _):
        greet(depth_peer(k), g)
        return 0

    lax.fori_loop(1, ND, greet_depth, 0)

    twin = g + 1 - 2 * core
    for k in range(4):
        greet(x_peer(k), twin)
    up, down = lax.rem(d + 1, ND), lax.rem(d + ND - 1, ND)
    right, left = lax.rem(g + 1, NG), lax.rem(g + NG - 1, NG)
    greet(d, right)
    greet(d, left)
    for dd in (up, down):
        for gg in (right, left):
            greet(dd, gg)

    row = iota((ROWS, LANES), 0)
    lane = iota((ROWS, LANES), 1)
    eye = one_hot(row == lane)
    perm = one_hot(lane == (row & 1) * C + (row >> 1))
    permt = one_hot(row == (lane & 1) * C + (lane >> 1))

    loads[0].wait()
    two = mw[pl.ds(2 * core, 2)].reshape(2 * C, C)
    wall[core, xd, zd] = dot(eye[:C, :C], two, 1, 1).astype(BF16)

    def weights_copy(n, k):
        ref = wall.at[core, xd, zd] if n == 0 else wall.at[core, xd]
        to = (z_peer(k), g) if n == 0 else (x_peer(k % 4), g if k < 4 else twin)
        return pltpu.make_async_remote_copy(
            ref, ref, pss.at[n, k], prs.at[n, k], device_id=to, device_id_type=MESH
        )

    def weights_from(n, k):
        if n == 0:
            ref = wall.at[core, xd, lax.rem(zd + 4 - k, 4)]
        else:
            ref = wall.at[core if k < 4 else 1 - core, lax.rem(xd + 8 - k, 4)]
        return pltpu.make_async_remote_copy(
            ref, ref, pss.at[n, k], prs.at[n, k], device_id=(d, twin), device_id_type=MESH
        )

    def weights_start(n):
        for k in range(1, 4 + 4 * n):
            weights_copy(n, k).start()

    def weights_wait(n):
        for k in range(1, 4 + 4 * n):
            weights_from(n, k).wait()

    def slab_copies(n, ts):
        mid = pl.ds(ROWS, ROWS)
        for i, (src, dst, dd) in enumerate([(1, CD + 1, down), (CD, 0, up)]):
            yield pltpu.make_async_remote_copy(
                ts.at[src, mid, :], ts.at[dst, mid, :], hss.at[n, i], hrs.at[n, i], device_id=(dd, g), device_id_type=MESH
            )

    def edge_copies(n):
        i = 2
        for side, gg in ((0, left), (1, right)):
            base = 64 * (1 - side)
            for src, rows, dst, dd in ((0, 32, 0, d), (16, 16, 32, up), (0, 16, 48, down)):
                yield pltpu.make_async_remote_copy(
                    eb.at[n, pl.ds(32 * side + src, rows), :],
                    rx.at[n, pl.ds(base + dst, rows), :],
                    hss.at[n, i],
                    hrs.at[n, i],
                    device_id=(dd, gg),
                    device_id_type=MESH,
                )
                i += 1


    def wait_vol(z, _):
        vol_load(z).wait()
        return 0

    lax.fori_loop(0, CD, wait_vol, 0)
    flat = vol.reshape(CD, ROWS, LANES)
    erow = iota((64, LANES), 0)
    elane = iota((64, LANES), 1)

    def edges_of(z, slab):
        pick = ((erow == z) & (elane == 0)) | ((erow == z + 32) & (elane == LANES - 1))
        return dot(one_hot(pick), slab, 1, 1)

    def edge_step(z, edge):
        return edge + edges_of(z, flat[z])

    eb[0] = lax.fori_loop(0, CD, edge_step, jnp.zeros((64, LANES), F32), unroll=12).astype(BF16)
    vs[1, ROWS : 2 * ROWS, :] = flat[0]
    vs[CD, ROWS : 2 * ROWS, :] = flat[CD - 1]
    loads[1].wait()


    def compress(i, _):
        r0 = pl.multiple_of(i * 32, 32)
        both = [flat[:, pl.ds(r0 + 16 * j, 16), :].reshape(CD * 16, LANES) for j in range(2)]
        res = dot(hk[...], jnp.concatenate(both, axis=1)).astype(BF16)
        for j in range(2):
            gb[:, pl.ds(r0 + 16 * j, 16), :] = res[:, LANES * j : LANES * (j + 1)].reshape(R, 16, LANES)
        return 0

    lax.fori_loop(0, ROWS // 32, compress, 0, unroll=4)

    for p in range(R // 2):
        pair = [dot(gb[2 * p + j], perm, 0, 0).reshape(ND, XO, LANES) for j in range(2)]
        fs[:, 16 * p : 16 * p + 16, :] = jnp.concatenate(pair, axis=1).astype(BF16)
    fr[d] = fs[d]


    def spectral_copy(src, dst, send, recv, t):
        return pltpu.make_async_remote_copy(
            src.at[t], dst.at[d], send.at[t], recv.at[d], device_id=(t, g), device_id_type=MESH
        )

    def spectral_from(src, dst, send, recv, t):
        return pltpu.make_async_remote_copy(
            src.at[t], dst.at[t], send.at[t], recv.at[t], device_id=(t, g), device_id_type=MESH
        )

    pl.semaphore_wait(barrier, ND - 1 + 4 + 2 + 4)
    weights_start(0)
    for c in edge_copies(0):
        c.start()
    for c in slab_copies(0, vs):
        c.start()

    def send_forward(j, _):
        spectral_copy(fs, fr, fss, frs, far_first(j)).start()
        return 0

    lax.fori_loop(0, ND - 1, send_forward, 0)

    def spread(ts, zi, slab):
        ts[zi, 0:ROWS, :] = pltpu.roll(slab, 1, 1)
        ts[zi, ROWS : 2 * ROWS, :] = slab
        ts[zi, 2 * ROWS : 3 * ROWS, :] = pltpu.roll(slab, LANES - 1, 1)

    def fill(z, _):
        spread(vs, z + 1, flat[z])
        return 0

    for z in (0, CD - 1):
        slab = flat[z]
        vs[z + 1, 0:ROWS, :] = pltpu.roll(slab, 1, 1)
        vs[z + 1, 2 * ROWS : 3 * ROWS, :] = pltpu.roll(slab, LANES - 1, 1)
    lax.fori_loop(1, CD - 1, fill, 0, unroll=11)
    loads[2].wait()
    loads[4].wait()

    def taps(t, _):
        a, e = t // 3, lax.rem(t, 3)

        def halves(w):
            w0, w1, w2 = w[a, 0, e], w[a, 1, e], w[a, 2, e]
            return jnp.concatenate([w1, w0], axis=0), jnp.concatenate([w2, w1], axis=0)

        lo, hi = halves(wc1)
        wa[t] = (dot(lo, permt[:C]) + dot(hi, permt[C:])).astype(BF16)
        lo, hi = halves(wc2)
        both = (dot(lo, eye[:C]) + dot(hi, eye[C:])).astype(BF16)
        wb[t] = dot(perm, both).astype(BF16)
        return 0

    lax.fori_loop(0, 9, taps, 0, unroll=3)


    def complete(n, ts):
        for c in slab_copies(n, ts):
            c.wait()
        for c in edge_copies(n):
            c.wait()
        for zi, there in ((0, d > 0), (CD + 1, d < ND - 1)):
            slab = ts[zi, ROWS : 2 * ROWS, :].astype(F32) * jnp.where(there, 1.0, 0.0)
            spread(ts, zi, slab.astype(BF16))
        sub = row & 63
        inside = jnp.where(row < 64, g, NG - 1 - g)
        slabs = jnp.where(sub < 32, 1, jnp.where(sub < 48, d, ND - 1 - d))
        keep = jnp.minimum(inside, slabs) > 0
        cells = jnp.where(keep, rx[n].astype(F32), 0.0).astype(BF16)
        columns = dot(eye, cells, 1, 1).astype(BF16)
        wrow = iota((ROWS, 2 * LANES), 0)
        wlane = iota((ROWS, 2 * LANES), 1)

        def patch(zi, _):
            rho = jnp.where(zi == 0, 39, jnp.where(zi == CD + 1, 48, zi - 1))
            put = ((wrow == rho) & (wlane == 0)) | ((wrow == rho + 64) & (wlane == 2 * LANES - 1))
            ins = dot(columns, one_hot(put)).astype(BF16)
            ts[zi, 0:ROWS, :] = jnp.where(lane == 0, ins[:, :LANES], ts[zi, 0:ROWS, :])
            ts[zi, 2 * ROWS : 3 * ROWS, :] = jnp.where(
                lane == LANES - 1, ins[:, LANES:], ts[zi, 2 * ROWS : 3 * ROWS, :]
            )
            return 0

        lax.fori_loop(0, CD + 2, patch, 0, unroll=13)

    def conv_pair(w, ts, z):
        lhs = jnp.concatenate([w[t] for t in range(9)], axis=1)
        rhs = [ts[pl.ds(z + j, 3)].reshape(9 * ROWS, LANES) for j in range(2)]
        return dot(lhs, jnp.concatenate(rhs, axis=1))

    weights_wait(0)
    weights_start(1)
    complete(0, vs)

    def first(i, edge):
        z = 2 * i
        hidden = gelu(conv_pair(wa, vs, z)).astype(BF16)
        for j in range(2):
            slab = hidden[:, LANES * j : LANES * (j + 1)]
            spread(hs, z + j + 1, slab)
            edge = edge + edges_of(z + j, slab)
        return edge

    eb[1] = lax.fori_loop(0, CD // 2, first, jnp.zeros((64, LANES), F32), unroll=2).astype(BF16)
    for c in slab_copies(1, hs):
        c.start()
    for c in edge_copies(1):
        c.start()

    half = iota((C, LANES), 1) < C

    def diagonal(i, _):
        owner = i // 2
        w = wall[lax.rem(i, 2), owner // 4, lax.rem(owner, 4)].astype(F32)
        turned = pltpu.roll(w, C, 1)
        top = [jnp.where(half, w, 0.0), jnp.where(half, turned, 0.0)]
        bottom = [jnp.where(half, 0.0, turned), jnp.where(half, 0.0, w)]
        bd[i, 0:C, :] = jnp.concatenate(top, axis=1).astype(BF16)
        bd[i, C : 2 * C, :] = jnp.concatenate(bottom, axis=1).astype(BF16)
        return 0


    loads[3].wait()
    loads[5].wait()

    def wait_forward(k, _):
        spectral_from(fs, fr, fss, frs, depth_peer(k)).wait()
        return 0

    lax.fori_loop(1, ND, wait_forward, 0)
    coef[...] = dot(gk[...], fr[...].reshape(ND * R * XO, LANES)).astype(BF16)

    weights_wait(1)
    lax.fori_loop(0, M // 2, diagonal, 0, unroll=4)
    def mix(i, _):
        rows = pl.ds(pl.multiple_of(16 * i, 16), 16)
        res = dot(coef[rows, :], bd[i])
        mixed[rows, :] = jnp.concatenate([res[:8, :LANES], res[8:, LANES:]], axis=0).astype(BF16)
        return 0

    lax.fori_loop(0, M // 2, mix, 0, unroll=8)
    def send_back(xs, count):
        n = 4 * R * XO
        rows = pl.ds(pl.multiple_of(xs * n, 16), n)
        bs[pl.ds(xs * 4, 4)] = dot(gkt[rows, :], mixed[...]).astype(BF16).reshape(4, R * XO, LANES)

        def step(j, _):
            far = half_z + (1 - j // 2) * (1 - 2 * half_z)
            spectral_copy(bs, br, bss, brs, xs * 4 + 2 * far + lax.rem(zd + j + 1, 2)).start()
            return 0

        lax.fori_loop(0, count, step, 0)

    for k in (2, 1, 3):
        send_back(lax.rem(xd + k, 4), 4)
    send_back(xd, 3)
    br[d] = bs[d]

    complete(1, hs)

    def second(i, _):
        z = 2 * i
        res = conv_pair(wb, hs, z)
        for j in range(2):
            acc[z + j] = flat[z + j].astype(F32) + res[:, LANES * j : LANES * (j + 1)]
        return 0

    lax.fori_loop(0, CD // 2, second, 0, unroll=2)

    loads[6].wait()

    def wait_back(k, _):
        spectral_from(bs, br, bss, brs, depth_peer(k)).wait()
        return 0

    lax.fori_loop(1, ND, wait_back, 0)
    for p in range(R // 2):
        pair = br[:, 16 * p : 16 * p + 16, :].astype(F32)
        for j in range(2):
            cols = pair[:, XO * j : XO * (j + 1)].reshape(LANES, ROWS).astype(BF16)
            gb[2 * p + j] = dot(perm, cols, 1, 1).astype(BF16)

    def expand(i, _):
        r0 = pl.multiple_of(i * 32, 32)
        both = [gb[:, pl.ds(r0 + 16 * j, 16), :].reshape(R * 16, LANES) for j in range(2)]
        res = dot(hkt[...], jnp.concatenate(both, axis=1))
        for j in range(2):
            rows = pl.ds(r0 + 16 * j, 16)
            total = acc[:, rows, :] + res[:, LANES * j : LANES * (j + 1)].reshape(CD, 16, LANES)
            res_out[:, rows, :] = total.astype(BF16)
            put_out(i, j).start()
        return 0

    def put_out(i, j):
        rows = pl.ds(pl.multiple_of(i * 32, 32) + 16 * j, 16)
        return pltpu.make_async_copy(res_out.at[:, rows, :], out.at[:, rows, :], out_sem.at[2 * i + j])

    lax.fori_loop(0, ROWS // 32, expand, 0, unroll=4)
    for i in range(ROWS // 32):
        for j in range(2):
            put_out(i, j).wait()


def local(volume, conv_first, conv_second, mode_weights):
    vmem = pltpu.VMEM
    dma = pltpu.SemaphoreType.DMA
    hbm = pl.BlockSpec(memory_space=pltpu.HBM)
    res = pl.pallas_call(
        kernel,
        out_shape=jax.ShapeDtypeStruct((CD, ROWS, LANES), BF16),
        in_specs=[hbm] * 8,
        out_specs=pl.BlockSpec(memory_space=pltpu.HBM),
        scratch_shapes=[
            vmem((CD, C, 2, LANES), BF16),
            vmem((3, 3, 3, C, C), BF16),
            vmem((3, 3, 3, C, C), BF16),
            vmem((4, C, C), BF16),
            vmem((R * 16, CD * 16), BF16),
            vmem((CD * 16, R * 16), BF16),
            vmem((M * XO, ND * R * XO), BF16),
            vmem((ND * R * XO, M * XO), BF16),
            vmem((CD + 2, 3 * ROWS, LANES), BF16),
            vmem((CD + 2, 3 * ROWS, LANES), BF16),
            vmem((9, ROWS, LANES), BF16),
            vmem((9, ROWS, LANES), BF16),
            vmem((CD, ROWS, LANES), F32),
            vmem((2, 64, LANES), BF16),
            vmem((2, ROWS, LANES), BF16),
            vmem((R, ROWS, LANES), BF16),
            vmem((ND, R * XO, LANES), BF16),
            vmem((ND, R * XO, LANES), BF16),
            vmem((ND, R * XO, LANES), BF16),
            vmem((ND, R * XO, LANES), BF16),
            vmem((M * XO, LANES), BF16),
            vmem((M * XO, LANES), BF16),
            vmem((2, 4, 4, C, LANES), BF16),
            vmem((M // 2, ROWS, 2 * LANES), BF16),
            vmem((CD, ROWS, LANES), BF16),
            dma((7,)),
            dma((CD,)),
            dma((ND,)),
            dma((ND,)),
            dma((ND,)),
            dma((ND,)),
            dma((2, 8)),
            dma((2, 8)),
            dma((2, 8)),
            dma((2, 8)),
            dma((8,)),
        ],
        compiler_params=pltpu.CompilerParams(
            collective_id=0, has_side_effects=True, vmem_limit_bytes=60 * 2**20
        ),
    )(volume, conv_first, conv_second, mode_weights, *constants())
    return res.reshape(CD, C, 2, LANES).transpose(1, 0, 2, 3)


def solution(mesh):
    placed = (P(None, "depth", None, "gx"), P(), P(), P("depth", None, None))
    return jax.shard_map(
        local, mesh=mesh, in_specs=placed, out_specs=P(None, "depth", None, "gx"), check_vma=False
    )
```
